32 devices in a mesh: mp: 4 (over y, x), item: 8 (over z, core).
Axes of the slice: x: 2, y: 2, z: 4, core: 2. Of those that a mesh axis runs over, the one named last changes fastest.
Arguments:
- response: int32 [8192, 16384], P('mp', 'item'), may hold values from 0 to 2
- difficulty: float32 [16384], P('item'), may hold values from -4 to 4
- ability: float32 [8192, 256], P('mp', 'item'), may hold values from -6 to 6
- ability_m: float32 [8192, 256], P('mp', 'item'), may hold values from -3 to 3
- ability_v: float32 [8192, 256], P('mp', 'item'), may hold values from 0.02 to 0.5
- discrim: float32 [16384, 256], P('item', 'mp'), may hold values from -0.375 to 0.375
- discrim_m: float32 [16384, 256], P('item', 'mp'), may hold values from -3 to 3
- discrim_v: float32 [16384, 256], P('item', 'mp'), may hold values from 0.02 to 0.5
Outputs:
- ability_new: float32 [8192, 256], P('mp', 'item')
- ability_m_new: float32 [8192, 256], P('mp', 'item')
- ability_v_new: float32 [8192, 256], P('mp', 'item')
- discrim_new: float32 [16384, 256], P('item', 'mp')
- discrim_m_new: float32 [16384, 256], P('item', 'mp')
- discrim_v_new: float32 [16384, 256], P('item', 'mp')
The draws below stay inside these ranges and needn't reach their ends.
Inputs may be any that keep to these rules, and one draw needn't show every extreme that they name: `response`: 0 marks an unobserved pair, 1 an observed wrong answer, 2 an observed right answer.
All inputs are finite; a program needn't handle non-finite values.
Results may differ from the reference program's by a relative error of at most 0.0012.
Values may be sent and summed in bfloat16 or wider, within the bound.
No kernel may reach another device: no remote copies, remote signals or barrier semaphores. Data moves between devices by JAX's collectives and lax.ppermute only.
A program may use at most 128 MiB of HBM per device.

```python
import math
import jax
import jax.numpy as jnp
from jax import lax

K = 256
CKPT_DEV = 2048
CKPTS = 8192
ITEMS = 16384
N_MP = 4


def touch_ends(values, own_key, smallest, high):
    shape = values.shape
    spot = [jax.random.randint(jax.random.fold_in(own_key, axis), (), 0, shape[axis]) for axis in range(len(shape))]
    values = values.at[tuple(spot)].set(smallest)
    longest = shape.index(max(shape))
    spot[longest] = (spot[longest] + 1) % shape[longest]
    return values.at[tuple(spot)].set(high)


def block_levels(stream_key, dims, cuts, least, largest):
    gain, own = 1.0, jax.random.fold_in(stream_key, 6)
    for axis_at, parts in cuts:
        draws = jnp.exp(jax.random.uniform(jax.random.fold_in(own, axis_at), (parts,), jnp.float32, least / len(cuts), largest / len(cuts)))
        gain = gain * jnp.repeat(draws, dims[axis_at] // parts).reshape([-1 if axis == axis_at else 1 for axis in range(len(dims))])
    return gain


def bell_draw(key, shape, scale, reach, shards=(), kind=jnp.bfloat16):
    array = jax.random.normal(key, shape, jnp.float32) * scale
    if len(shards) > 0:
        array = block_levels(key, shape, shards, -0.22, 0.18) * array
    return jnp.clip(array, min=-reach, max=reach).astype(kind)


def setup_inputs(seed: int = 0) -> dict:
    keys = jax.random.split(jax.random.key(seed), 9)
    response = touch_ends(jax.random.randint(keys[0], (CKPTS, ITEMS), 0, 3), jax.random.fold_in(keys[0], 1), 0, 2).astype(jnp.int32)
    difficulty = bell_draw(keys[1], (ITEMS,), 1.0, 4.0, ((0, 8),), jnp.float32)
    ability = bell_draw(keys[2], (CKPTS, K), 1.0, 6.0, ((0, 4), (1, 8)), jnp.float32)
    ability_m = bell_draw(keys[3], (CKPTS, K), 0.4, 3.0, ((0, 4), (1, 8)), jnp.float32)
    ability_v = jnp.clip(jnp.exp(math.log(0.5) - 3.218876 * jax.random.uniform(keys[4], (CKPTS, K), jnp.float32) ** block_levels(keys[4], (CKPTS, K), ((0, 4), (1, 8)), -0.2, 0.2)), 0.02, 0.5)
    discrim = bell_draw(keys[5], (ITEMS, K), K ** -0.5, 0.375, ((0, 8), (1, 4)), jnp.float32)
    discrim_m = bell_draw(keys[6], (ITEMS, K), 0.4, 3.0, ((0, 8), (1, 4)), jnp.float32)
    discrim_v = jnp.clip(jnp.exp(math.log(0.5) - 3.218876 * jax.random.uniform(keys[7], (ITEMS, K), jnp.float32) ** block_levels(keys[7], (ITEMS, K), ((0, 8), (1, 4)), -0.2, 0.2)), 0.02, 0.5)
    return dict(response=response, difficulty=difficulty, ability=ability, ability_m=ability_m, ability_v=ability_v, discrim=discrim, discrim_m=discrim_m, discrim_v=discrim_v)


beta_one = 0.9
beta_two = 0.999
corr_one = 1.0 - 0.9 ** 10
corr_two = 1.0 - 0.999 ** 10
adam_eps = 1e-08

def adam_update(factor, moment, second, gradient, step_rate):
    moment_new = beta_one * moment + (1.0 - beta_one) * gradient
    second_new = beta_two * second + (1.0 - beta_two) * gradient * gradient
    update = moment_new / corr_one / (jnp.sqrt(second_new / corr_two) + adam_eps)
    return (factor - step_rate * update, moment_new, second_new)

def reference(response, difficulty, ability, ability_m, ability_v, discrim, discrim_m, discrim_v):
    ability_bf = ability.astype(jnp.bfloat16)
    discrim_bf = discrim.astype(jnp.bfloat16)
    discrim_wide = discrim_bf.astype(jnp.float32)
    ability_blocks = ability_bf.reshape(N_MP, CKPT_DEV, K)
    response_blocks = response.reshape(N_MP, CKPT_DEV, ITEMS)

    def block_step(total, pieces):
        rows_bf, rows_response = pieces
        logits = jnp.dot(rows_bf, discrim_bf.T, preferred_element_type=jnp.float32) + difficulty[None, :]
        correct = (rows_response == 2).astype(jnp.float32)
        residual = jnp.where(rows_response > 0, jax.nn.sigmoid(logits) - correct, jnp.float32(0.0))
        grad_rows = jnp.dot(residual, discrim_wide, precision=lax.Precision.HIGHEST)
        total = total + jnp.dot(residual.T, rows_bf.astype(jnp.float32), precision=lax.Precision.HIGHEST)
        return (total, grad_rows)
    start_total = jnp.zeros((ITEMS, K), jnp.float32)
    discrim_sum, ability_rows = lax.scan(block_step, start_total, (ability_blocks, response_blocks))
    ability_grad = ability_rows.reshape(CKPTS, K) * math.sqrt(K / ITEMS)
    discrim_grad = discrim_sum * math.sqrt(1.0 / CKPTS)
    ability_new, ability_m_new, ability_v_new = adam_update(ability, ability_m, ability_v, ability_grad, 0.05)
    discrim_new, discrim_m_new, discrim_v_new = adam_update(discrim, discrim_m, discrim_v, discrim_grad, 0.01)
    return (ability_new, ability_m_new, ability_v_new, discrim_new, discrim_m_new, discrim_v_new)
```

```python
import functools
import math

import jax
import jax.numpy as jnp
from jax import lax
from jax.experimental import pallas as pl
from jax.experimental.pallas import tpu as pltpu
from jax.sharding import PartitionSpec as P

beta_one = 0.9
beta_two = 0.999
corr_one = 1.0 - 0.9**10
corr_two = 1.0 - 0.999**10
adam_eps = 1e-08

BF = jnp.bfloat16
F32 = jnp.float32
VMEM_BYTES = 52 * 2**20
ROW_TILE = 512
COL_TILE = 512


def adam_update(factor, moment, second, gradient, step_rate):
    moment_new = beta_one * moment + (1.0 - beta_one) * gradient
    second_new = beta_two * second + (1.0 - beta_two) * gradient * gradient
    update = moment_new / corr_one / (jnp.sqrt(second_new / corr_two) + adam_eps)
    return (factor - step_rate * update, moment_new, second_new)


def cast_kernel(a_ref, d_ref, a_out, d_out):
    a_out[...] = a_ref[...].astype(BF)
    d_out[...] = d_ref[...].astype(BF)


def cast_both(a, d):
    return pl.pallas_call(
        cast_kernel,
        out_shape=(jax.ShapeDtypeStruct(a.shape, BF), jax.ShapeDtypeStruct(d.shape, BF)),
        name="cast_factors",
    )(a, d)


def swap_item(n_item, mask):
    return [(i, i ^ mask) for i in range(n_item)]


def swap_mp(n_mp, n_item, mask):
    pairs = []
    for m in range(n_mp):
        for i in range(n_item):
            other = mask if i % 2 == 0 or n_mp < 4 else {1: 2, 2: 1}.get(mask, mask)
            pairs.append((m * n_item + i, (m ^ other) * n_item + i))
    return pairs


def mp_masks(n_mp):
    swap = lambda x: x if n_mp < 4 else (x & ~3) | ((x & 1) << 1) | ((x >> 1) & 1)
    return [(x, swap(x)) for x in range(n_mp)]


def gather_mp(d, n_mp, n_item):
    blocks = [d]
    bit = 1
    while bit < n_mp:
        perm = swap_mp(n_mp, n_item, bit)
        blocks += [lax.ppermute(b, ("mp", "item"), perm) for b in blocks]
        bit *= 2
    return blocks


def gather_item(a, n_item):
    chips = n_item // 2
    mine = [a] + [lax.ppermute(a, "item", swap_item(n_item, 2 * x)) for x in range(1, chips)]
    theirs = [lax.ppermute(b, "item", swap_item(n_item, 1)) for b in mine]
    return mine + theirs


def grad_kernel(n_mp, n_item, *refs):
    chips = n_item // 2
    a_in, refs = refs[:n_item], refs[n_item:]
    d_in, refs = refs[:n_mp], refs[n_mp:]
    diff_ref, r_hbm = refs[:2]
    keep_ref, give_ref, *h_out = refs[2 : 4 + n_mp]
    at, dt, resp, rs, gs, acc, sem_in, sem_r = refs[4 + n_mp :]
    k, rows = at.shape
    cols = dt.shape[1]
    ka, kd = k // n_item, k // n_mp
    tiles = rows // ROW_TILE

    item = lax.axis_index("item")
    m = lax.axis_index("mp")
    chip, core = item // 2, lax.rem(item, 2)

    def owner_item(x, flip):
        return (chip ^ x) * 2 + (core ^ flip)

    copies = []
    for q, (x, flip) in enumerate((x, f) for f in range(2) for x in range(chips)):
        off = pl.multiple_of(owner_item(x, flip) * ka, ka)
        copies.append(pltpu.make_async_copy(a_in[q], at.at[pl.ds(off, ka)], sem_in.at[q]))
    for q, (even, odd) in enumerate(mp_masks(n_mp)):
        off = pl.multiple_of((m ^ jnp.where(core == 0, even, odd)) * kd, kd)
        copies.append(pltpu.make_async_copy(d_in[q], dt.at[pl.ds(off, kd)], sem_in.at[n_item + q]))
    loads = []
    for t in range(tiles):
        rng = pl.ds(t * ROW_TILE, ROW_TILE)
        loads.append(pltpu.make_async_copy(r_hbm.at[rng], resp.at[rng], sem_r.at[t]))
    for c in copies:
        c.start()
    for c in loads:
        c.start()
    for c in copies:
        c.wait()

    n_cols = cols // COL_TILE
    sub = ROW_TILE // n_cols
    for t in range(tiles + 1):
        if t < tiles:
            loads[t].wait()
            rng = slice(t * ROW_TILE, (t + 1) * ROW_TILE)
            half = (at[:, rng].astype(F32) * 0.5).T.astype(BF)
        if t > 0:
            old = slice((t - 1) * ROW_TILE, t * ROW_TILE)
            at_old = at[:, old]
        for c in range(n_cols):
            cr = slice(c * COL_TILE, (c + 1) * COL_TILE)
            if t < tiles:
                lg = jnp.dot(half, dt[:, cr], preferred_element_type=F32) + 0.5 * diff_ref[:, cr]
                r = resp[rng, cr]
                sign = jnp.where(r == 2, -1.0, 1.0)
                rs[t % 2, :, cr] = jnp.where(r == 0, 0.0, jnp.tanh(lg) + sign).astype(BF)
            if t > 0:
                p = (t - 1) % 2
                h = jnp.dot(at_old, rs[p, :, cr], preferred_element_type=F32)
                if t == 1:
                    acc[:, cr] = h
                else:
                    acc[:, cr] += h
                g = lax.dot_general(
                    rs[p, c * sub : (c + 1) * sub, :],
                    dt[...],
                    (((1,), (1,)), ((), ())),
                    preferred_element_type=F32,
                )
                lo = (t - 1) * ROW_TILE + c * sub
                gs[:, lo : lo + sub] = g.T

    for x in range(chips):
        dst = pl.ds(x * ka, ka)
        keep_ref[dst, :] = gs[pl.ds(pl.multiple_of(owner_item(x, 0) * ka, ka), ka), :]
        give_ref[dst, :] = gs[pl.ds(pl.multiple_of(owner_item(x, 1) * ka, ka), ka), :].astype(BF)
    for x in range(n_mp):
        h = acc[pl.ds(pl.multiple_of((m ^ x) * kd, kd), kd), :]
        h_out[x][...] = h.astype(h_out[x].dtype)


def gradients(a_blocks, d_blocks, difficulty, response, n_mp, n_item):
    ka, rows = a_blocks[0].shape
    kd, cols = d_blocks[0].shape
    k = ka * n_item
    tiles = rows // ROW_TILE
    flops = 3 * 2 * rows * cols * k
    shape = jax.ShapeDtypeStruct
    any_spec = pl.BlockSpec(memory_space=pl.ANY)
    vmem = pl.BlockSpec(memory_space=pltpu.VMEM)
    outs = [shape((k // 2, rows), F32), shape((k // 2, rows), BF), shape((kd, cols), F32)]
    outs += [shape((kd, cols), BF)] * (n_mp - 1)
    return pl.pallas_call(
        functools.partial(grad_kernel, n_mp, n_item),
        out_shape=outs,
        in_specs=[any_spec] * (n_item + n_mp) + [vmem, any_spec],
        out_specs=[vmem] * len(outs),
        scratch_shapes=[
            pltpu.VMEM((k, rows), BF),
            pltpu.VMEM((k, cols), BF),
            pltpu.VMEM((rows, cols), jnp.int32),
            pltpu.VMEM((2, ROW_TILE, cols), BF),
            pltpu.VMEM((k, rows), F32),
            pltpu.VMEM((k, cols), F32),
            pltpu.SemaphoreType.DMA((n_item + n_mp,)),
            pltpu.SemaphoreType.DMA((tiles,)),
        ],
        compiler_params=pltpu.CompilerParams(vmem_limit_bytes=VMEM_BYTES),
        cost_estimate=pl.CostEstimate(
            flops=flops, bytes_accessed=4 * rows * cols, transcendentals=rows * cols
        ),
        name="residual_gradients",
    )(*a_blocks, *d_blocks, difficulty, response)


def pair_kernel(ka, keep_ref, got_ref, own_ref, *outs):
    own_ref[...] = keep_ref[:ka, :] + got_ref[:ka, :].astype(F32)
    for q, out in enumerate(outs):
        rng = slice((q + 1) * ka, (q + 2) * ka)
        out[...] = (keep_ref[rng, :] + got_ref[rng, :].astype(F32)).astype(BF)


def pair_sum(keep, got, chips):
    ka, rows = keep.shape[0] // chips, keep.shape[1]
    shape = jax.ShapeDtypeStruct
    return pl.pallas_call(
        functools.partial(pair_kernel, ka),
        out_shape=[shape((ka, rows), F32)] + [shape((ka, rows), BF)] * (chips - 1),
        name="core_pair_sum",
    )(keep, got)


def shards(response, difficulty, ability, ability_m, ability_v, discrim, discrim_m, discrim_v):
    n_item, n_mp = lax.axis_size("item"), lax.axis_size("mp")
    chips = n_item // 2
    rows, cols = response.shape
    k = discrim.shape[1] * n_mp
    items_total, ckpts_total = cols * n_item, rows * n_mp
    a_bf, d_bf = cast_both(ability.T, discrim.T)
    d_blocks = gather_mp(d_bf, n_mp, n_item)
    a_blocks = gather_item(a_bf, n_item)
    keep, give, *h = gradients(
        a_blocks, d_blocks, difficulty.reshape(1, cols), response, n_mp, n_item
    )
    h_sum = h[0]
    h_got = [
        lax.ppermute(h[x], "mp", [(i, i ^ x) for i in range(n_mp)]) for x in range(1, n_mp)
    ]
    got = lax.ppermute(give, "item", swap_item(n_item, 1))
    g_sum, *g = pair_sum(keep, got, chips)
    g_got = [
        lax.ppermute(g[x - 1], "item", swap_item(n_item, 2 * x)) for x in range(1, chips)
    ]
    for b in g_got:
        g_sum = g_sum + b.astype(F32)
    for b in h_got:
        h_sum = h_sum + b.astype(F32)
    a_out = adam_update(
        ability.T, ability_m.T, ability_v.T, g_sum * (0.5 * math.sqrt(k / items_total)), 0.05
    )
    d_out = adam_update(
        discrim.T, discrim_m.T, discrim_v.T, h_sum * (0.5 * math.sqrt(1.0 / ckpts_total)), 0.01
    )
    return tuple(x.T for x in a_out + d_out)


def solution(mesh):
    a_spec, d_spec = P("mp", "item"), P("item", "mp")
    return jax.shard_map(
        shards,
        mesh=mesh,
        in_specs=(a_spec, P("item")) + (a_spec,) * 3 + (d_spec,) * 3,
        out_specs=(a_spec,) * 3 + (d_spec,) * 3,
        check_vma=False,
    )
```

```python
import functools
import math

import jax
import jax.numpy as jnp
from jax import lax
from jax.experimental import pallas as pl
from jax.experimental.pallas import tpu as pltpu
from jax.sharding import PartitionSpec as P

beta_one = 0.9
beta_two = 0.999
corr_one = 1.0 - 0.9**10
corr_two = 1.0 - 0.999**10
adam_eps = 1e-08

BF = jnp.bfloat16
F32 = jnp.float32
VMEM_BYTES = 34 * 2**20
SMALL_VMEM = 8 * 2**20
ROW_TILE = 512
COL_TILE = 512


def adam_update(factor, moment, second, gradient, step_rate):
    moment_new = beta_one * moment + (1.0 - beta_one) * gradient
    second_new = beta_two * second + (1.0 - beta_two) * gradient * gradient
    update = moment_new / corr_one / (jnp.sqrt(second_new / corr_two) + adam_eps)
    return (factor - step_rate * update, moment_new, second_new)


def cast_kernel(x_ref, out_ref):
    out_ref[...] = x_ref[...].astype(BF)


def cast(x):
    return pl.pallas_call(
        cast_kernel,
        out_shape=jax.ShapeDtypeStruct(x.shape, BF),
        compiler_params=pltpu.CompilerParams(vmem_limit_bytes=SMALL_VMEM),
        name="cast_factor",
    )(x)


def swap_item(n_item, mask):
    return [(i, i ^ mask) for i in range(n_item)]


def swap_mp(n_mp, n_item, mask):
    pairs = []
    for m in range(n_mp):
        for i in range(n_item):
            other = mask if i % 2 == 0 or n_mp < 4 else {1: 2, 2: 1}.get(mask, mask)
            pairs.append((m * n_item + i, (m ^ other) * n_item + i))
    return pairs


def mp_masks(n_mp):
    swap = lambda x: x if n_mp < 4 else (x & ~3) | ((x & 1) << 1) | ((x >> 1) & 1)
    return [(x, swap(x)) for x in range(n_mp)]


def gather_mp(d, n_mp, n_item):
    blocks = [d]
    bit = 1
    while bit < n_mp:
        perm = swap_mp(n_mp, n_item, bit)
        blocks += [lax.ppermute(b, ("mp", "item"), perm) for b in blocks]
        bit *= 2
    return blocks


def gather_item(a, n_item):
    chips = n_item // 2
    mine = [a] + [lax.ppermute(a, "item", swap_item(n_item, 2 * x)) for x in range(1, chips)]
    theirs = [lax.ppermute(b, "item", swap_item(n_item, 1)) for b in mine]
    return mine + theirs


def grad_kernel(n_mp, n_item, *refs):
    chips = n_item // 2
    a_in, refs = refs[:n_item], refs[n_item:]
    d_in, refs = refs[:n_mp], refs[n_mp:]
    diff_ref, r_hbm = refs[:2]
    keep_ref, give_ref, *h_out = refs[2 : 4 + n_mp]
    at, dt, resp, rs, gs, acc, sem_in, sem_r = refs[4 + n_mp :]
    k, rows = at.shape
    cols = dt.shape[1]
    ka, kd = k // n_item, k // n_mp
    tiles = rows // ROW_TILE

    item = lax.axis_index("item")
    m = lax.axis_index("mp")
    chip, core = item // 2, lax.rem(item, 2)

    def owner_item(x, flip):
        return (chip ^ x) * 2 + (core ^ flip)

    copies = []
    for q, (x, flip) in enumerate((x, f) for f in range(2) for x in range(chips)):
        off = pl.multiple_of(owner_item(x, flip) * ka, ka)
        copies.append(pltpu.make_async_copy(a_in[q], at.at[pl.ds(off, ka)], sem_in.at[q]))
    for q, (even, odd) in enumerate(mp_masks(n_mp)):
        off = pl.multiple_of((m ^ jnp.where(core == 0, even, odd)) * kd, kd)
        copies.append(pltpu.make_async_copy(d_in[q], dt.at[pl.ds(off, kd)], sem_in.at[n_item + q]))

    def load(t):
        rng = pl.ds(pl.multiple_of(t * ROW_TILE, ROW_TILE), ROW_TILE)
        return pltpu.make_async_copy(r_hbm.at[rng], resp.at[rng], sem_r.at[t])

    for c in copies:
        c.start()
    for t in range(tiles):
        load(t).start()
    for c in copies:
        c.wait()

    acc[...] = jnp.zeros_like(acc)

    def step(t, carry):
        rng = pl.ds(pl.multiple_of(t * ROW_TILE, ROW_TILE), ROW_TILE)
        load(t).wait()
        a_tile = at[:, rng]
        half = (a_tile.astype(F32) * 0.5).T.astype(BF)
        for c in range(0, cols, COL_TILE):
            cr = slice(c, c + COL_TILE)
            lg = jnp.dot(half, dt[:, cr], preferred_element_type=F32) + 0.5 * diff_ref[:, cr]
            r = resp[rng, cr]
            sign = jnp.where(r == 2, -1.0, 1.0)
            rs[:, cr] = jnp.where(r == 0, 0.0, jnp.tanh(lg) + sign).astype(BF)
        gs[:, rng] = lax.dot_general(
            dt[...], rs[...], (((1,), (1,)), ((), ())), preferred_element_type=F32
        )
        for c in range(0, cols, COL_TILE):
            cr = slice(c, c + COL_TILE)
            acc[:, cr] += jnp.dot(a_tile, rs[:, cr], preferred_element_type=F32)
        return carry

    lax.fori_loop(0, tiles, step, 0)

    for x in range(chips):
        dst = pl.ds(x * ka, ka)
        keep_ref[dst, :] = gs[pl.ds(pl.multiple_of(owner_item(x, 0) * ka, ka), ka), :]
        give_ref[dst, :] = gs[pl.ds(pl.multiple_of(owner_item(x, 1) * ka, ka), ka), :].astype(BF)
    for x in range(n_mp):
        h = acc[pl.ds(pl.multiple_of((m ^ x) * kd, kd), kd), :]
        h_out[x][...] = h.astype(h_out[x].dtype)


def gradients(a_blocks, d_blocks, difficulty, response, n_mp, n_item):
    ka, rows = a_blocks[0].shape
    kd, cols = d_blocks[0].shape
    k = ka * n_item
    tiles = rows // ROW_TILE
    flops = 3 * 2 * rows * cols * k
    shape = jax.ShapeDtypeStruct
    any_spec = pl.BlockSpec(memory_space=pl.ANY)
    vmem = pl.BlockSpec(memory_space=pltpu.VMEM)
    outs = [shape((k // 2, rows), F32), shape((k // 2, rows), BF), shape((kd, cols), F32)]
    outs += [shape((kd, cols), BF)] * (n_mp - 1)
    return pl.pallas_call(
        functools.partial(grad_kernel, n_mp, n_item),
        out_shape=outs,
        in_specs=[any_spec] * (n_item + n_mp) + [vmem, any_spec],
        out_specs=[vmem] * len(outs),
        scratch_shapes=[
            pltpu.VMEM((k, rows), BF),
            pltpu.VMEM((k, cols), BF),
            pltpu.VMEM((rows, cols), jnp.int32),
            pltpu.VMEM((ROW_TILE, cols), BF),
            pltpu.VMEM((k, rows), F32),
            pltpu.VMEM((k, cols), F32),
            pltpu.SemaphoreType.DMA((n_item + n_mp,)),
            pltpu.SemaphoreType.DMA((tiles,)),
        ],
        compiler_params=pltpu.CompilerParams(vmem_limit_bytes=VMEM_BYTES),
        cost_estimate=pl.CostEstimate(
            flops=flops, bytes_accessed=4 * rows * cols, transcendentals=rows * cols
        ),
        name="residual_gradients",
    )(*a_blocks, *d_blocks, difficulty, response)


def pair_kernel(ka, keep_ref, got_ref, own_ref, *outs):
    own_ref[...] = keep_ref[:ka, :] + got_ref[:ka, :].astype(F32)
    for q, out in enumerate(outs):
        rng = slice((q + 1) * ka, (q + 2) * ka)
        out[...] = (keep_ref[rng, :] + got_ref[rng, :].astype(F32)).astype(BF)


def pair_sum(keep, got, chips):
    ka, rows = keep.shape[0] // chips, keep.shape[1]
    shape = jax.ShapeDtypeStruct
    return pl.pallas_call(
        functools.partial(pair_kernel, ka),
        out_shape=[shape((ka, rows), F32)] + [shape((ka, rows), BF)] * (chips - 1),
        compiler_params=pltpu.CompilerParams(vmem_limit_bytes=SMALL_VMEM),
        name="core_pair_sum",
    )(keep, got)


def adam_kernel(n_sums, scale, rate, *refs):
    sums, (x_ref, m_ref, v_ref, x_out, m_out, v_out) = refs[:n_sums], refs[n_sums:]
    g = sums[0][...]
    for part in sums[1:]:
        g = g + part[...].astype(F32)
    x_out[...], m_out[...], v_out[...] = adam_update(
        x_ref[...], m_ref[...], v_ref[...], g * scale, rate
    )


def adam(sums, x, m, v, scale, rate):
    return pl.pallas_call(
        functools.partial(adam_kernel, len(sums), scale, rate),
        out_shape=[jax.ShapeDtypeStruct(x.shape, F32)] * 3,
        compiler_params=pltpu.CompilerParams(vmem_limit_bytes=SMALL_VMEM),
        name="adam",
    )(*sums, x, m, v)


def shards(response, difficulty, ability, ability_m, ability_v, discrim, discrim_m, discrim_v):
    n_item, n_mp = lax.axis_size("item"), lax.axis_size("mp")
    chips = n_item // 2
    rows, cols = response.shape
    k = discrim.shape[1] * n_mp
    items_total, ckpts_total = cols * n_item, rows * n_mp
    a_t, d_t = ability.T, discrim.T
    a_bf = cast(a_t)
    a_bf, d_late = lax.optimization_barrier((a_bf, d_t))
    a_blocks = gather_item(a_bf, n_item)
    d_blocks = gather_mp(cast(d_late), n_mp, n_item)
    keep, give, *h = gradients(
        a_blocks, d_blocks, difficulty.reshape(1, cols), response, n_mp, n_item
    )

    def swap_h(x):
        return lax.ppermute(h[x], "mp", [(i, i ^ x) for i in range(n_mp)])

    h_got = [swap_h(1)]
    got = lax.ppermute(give, "item", swap_item(n_item, 1))
    g_sum, *g = pair_sum(keep, got, chips)
    g[0], *h[2:] = lax.optimization_barrier((g[0], *h[2:]))
    g_got = [
        lax.ppermute(g[x - 1], "item", swap_item(n_item, 2 * x)) for x in range(1, chips)
    ]
    h_got += [swap_h(x) for x in range(2, n_mp)]
    d_out = adam(
        [h[0]] + h_got, d_t, discrim_m.T, discrim_v.T, 0.5 * math.sqrt(1.0 / ckpts_total), 0.01
    )
    a_out = adam(
        [g_sum] + g_got, a_t, ability_m.T, ability_v.T, 0.5 * math.sqrt(k / items_total), 0.05
    )
    return tuple(x.T for x in (*a_out, *d_out))


def solution(mesh):
    a_spec, d_spec = P("mp", "item"), P("item", "mp")
    return jax.shard_map(
        shards,
        mesh=mesh,
        in_specs=(a_spec, P("item")) + (a_spec,) * 3 + (d_spec,) * 3,
        out_specs=(a_spec,) * 3 + (d_spec,) * 3,
        check_vma=False,
    )
```

```python
import functools
import math

import jax
import jax.numpy as jnp
from jax import lax
from jax.experimental import pallas as pl
from jax.experimental.pallas import tpu as pltpu
from jax.sharding import PartitionSpec as P

beta_one = 0.9
beta_two = 0.999
corr_one = 1.0 - 0.9**10
corr_two = 1.0 - 0.999**10
adam_eps = 1e-08

BF = jnp.bfloat16
F32 = jnp.float32
VMEM_BYTES = 34 * 2**20
SMALL_VMEM = 8 * 2**20
ROW_TILE = 512
COL_TILE = 512


def adam_update(factor, moment, second, gradient, step_rate):
    moment_new = beta_one * moment + (1.0 - beta_one) * gradient
    second_new = beta_two * second + (1.0 - beta_two) * gradient * gradient
    update = moment_new / corr_one / (jnp.sqrt(second_new / corr_two) + adam_eps)
    return (factor - step_rate * update, moment_new, second_new)


def prepare_kernel(a_ref, d_ref, a_out, d_out):
    a_out[...] = a_ref[...].astype(BF)
    d_out[...] = d_ref[...].astype(BF)


def prepare(a, d):
    shape = jax.ShapeDtypeStruct
    return pl.pallas_call(
        prepare_kernel,
        out_shape=(shape(a.shape, BF), shape(d.shape, BF)),
        compiler_params=pltpu.CompilerParams(vmem_limit_bytes=SMALL_VMEM),
        name="prepare",
    )(a, d)


def swap_item(n_item, mask):
    return [(i, i ^ mask) for i in range(n_item)]


def swap_mp(n_mp, n_item, even, odd):
    return [
        (m * n_item + i, (m ^ (odd if i % 2 else even)) * n_item + i)
        for m in range(n_mp)
        for i in range(n_item)
    ]


def chip_basis(chips):
    return [2**j - 1 for j in range(chips.bit_length() - 1, 0, -1)]


def mp_basis(n_mp):
    bits = [2**j for j in range(n_mp.bit_length() - 1)]
    return list(zip(bits, bits[1::-1] + bits[2:]))


def span(basis):
    masks = [0] if not basis or isinstance(basis[0], int) else [(0, 0)]
    for b in basis:
        if isinstance(b, int):
            masks += [x ^ b for x in masks]
        else:
            masks += [(x ^ b[0], y ^ b[1]) for x, y in masks]
    return masks


def gather(block, basis, send):
    blocks = [block]
    for b in basis:
        blocks += [send(x, b) for x in blocks]
    return blocks


def grad_kernel(n_mp, n_item, *refs):
    chips = n_item // 2
    a_in, refs = refs[:n_item], refs[n_item:]
    d_in, refs = refs[:n_mp], refs[n_mp:]
    bias_ref, r_hbm = refs[:2]
    keep_ref, give_ref, *h_out = refs[2 : 4 + n_mp]
    at, dt, resp, rs, gs, acc, sem_in, sem_r = refs[4 + n_mp :]
    k, rows = at.shape
    cols = dt.shape[1]
    ka, kd = k // n_item, k // n_mp
    tiles = rows // ROW_TILE

    item = lax.axis_index("item")
    m = lax.axis_index("mp")
    chip, core = item // 2, lax.rem(item, 2)

    def owner_item(x, flip):
        return (chip ^ x) * 2 + (core ^ flip)

    copies = []
    for q, (x, flip) in enumerate((x, f) for f in range(2) for x in span(chip_basis(chips))):
        off = pl.multiple_of(owner_item(x, flip) * ka, ka)
        copies.append(pltpu.make_async_copy(a_in[q], at.at[pl.ds(off, ka)], sem_in.at[q]))
    for q, (even, odd) in enumerate(span(mp_basis(n_mp))):
        off = pl.multiple_of((m ^ jnp.where(core == 0, even, odd)) * kd, kd)
        copies.append(pltpu.make_async_copy(d_in[q], dt.at[pl.ds(off, kd)], sem_in.at[n_item + q]))

    def load(t):
        rng = pl.ds(pl.multiple_of(t * ROW_TILE, ROW_TILE), ROW_TILE)
        return pltpu.make_async_copy(r_hbm.at[rng], resp.at[rng], sem_r.at[t])

    for c in copies:
        c.start()
    for t in range(tiles):
        load(t).start()
    for c in copies:
        c.wait()

    acc[...] = jnp.zeros_like(acc)

    def step(t, carry):
        rng = pl.ds(pl.multiple_of(t * ROW_TILE, ROW_TILE), ROW_TILE)
        load(t).wait()
        a_tile = at[:, rng]
        half = (a_tile.astype(F32) * 0.5).T.astype(BF)
        for c in range(0, cols, COL_TILE):
            cr = slice(c, c + COL_TILE)
            lg = jnp.dot(half, dt[:, cr], preferred_element_type=F32) + bias_ref[:, cr]
            r = resp[rng, cr]
            sign = jnp.where(r == 2, -1.0, 1.0)
            rs[:, cr] = jnp.where(r == 0, 0.0, jnp.tanh(lg) + sign).astype(BF)
        gs[:, rng] = lax.dot_general(
            dt[...], rs[...], (((1,), (1,)), ((), ())), preferred_element_type=F32
        )
        for c in range(0, cols, COL_TILE):
            cr = slice(c, c + COL_TILE)
            acc[:, cr] += jnp.dot(a_tile, rs[:, cr], preferred_element_type=F32)
        return carry

    lax.fori_loop(0, tiles, step, 0)

    for x in range(chips):
        dst = pl.ds(x * ka, ka)
        keep_ref[dst, :] = gs[pl.ds(pl.multiple_of(owner_item(x, 0) * ka, ka), ka), :]
        give_ref[dst, :] = gs[pl.ds(pl.multiple_of(owner_item(x, 1) * ka, ka), ka), :].astype(BF)
    for x in range(n_mp):
        h = acc[pl.ds(pl.multiple_of((m ^ x) * kd, kd), kd), :]
        h_out[x][...] = h.astype(h_out[x].dtype)


def gradients(a_blocks, d_blocks, bias, response, n_mp, n_item):
    ka, rows = a_blocks[0].shape
    kd, cols = d_blocks[0].shape
    k = ka * n_item
    flops = 3 * 2 * rows * cols * k
    shape = jax.ShapeDtypeStruct
    any_spec = pl.BlockSpec(memory_space=pl.ANY)
    vmem = pl.BlockSpec(memory_space=pltpu.VMEM)
    outs = [shape((k // 2, rows), F32), shape((k // 2, rows), BF)]
    outs += [shape((kd, cols), BF if q else F32) for q in range(n_mp)]
    return pl.pallas_call(
        functools.partial(grad_kernel, n_mp, n_item),
        out_shape=outs,
        in_specs=[any_spec] * (n_item + n_mp) + [vmem, any_spec],
        out_specs=[vmem] * len(outs),
        scratch_shapes=[
            pltpu.VMEM((k, rows), BF),
            pltpu.VMEM((k, cols), BF),
            pltpu.VMEM((rows, cols), jnp.int32),
            pltpu.VMEM((ROW_TILE, cols), BF),
            pltpu.VMEM((k, rows), F32),
            pltpu.VMEM((k, cols), F32),
            pltpu.SemaphoreType.DMA((n_item + n_mp,)),
            pltpu.SemaphoreType.DMA((rows // ROW_TILE,)),
        ],
        compiler_params=pltpu.CompilerParams(vmem_limit_bytes=VMEM_BYTES),
        cost_estimate=pl.CostEstimate(
            flops=flops, bytes_accessed=4 * rows * cols, transcendentals=rows * cols
        ),
        name="residual_gradients",
    )(*a_blocks, *d_blocks, bias, response)


def pair_kernel(keep_ref, got_ref, *outs):
    ka = outs[0].shape[0]
    for x, out in enumerate(outs):
        rng = slice(x * ka, (x + 1) * ka)
        out[...] = (keep_ref[rng, :] + got_ref[rng, :].astype(F32)).astype(out.dtype)


def pair_sum(keep, got, chips):
    shape = (keep.shape[0] // chips, keep.shape[1])
    return pl.pallas_call(
        pair_kernel,
        out_shape=[jax.ShapeDtypeStruct(shape, BF if x else F32) for x in range(chips)],
        compiler_params=pltpu.CompilerParams(vmem_limit_bytes=SMALL_VMEM),
        name="core_pair_sum",
    )(keep, got)


def adam_kernel(plan, *refs):
    n_in = sum(n for n, _, _ in plan) + 3 * len(plan)
    ins, outs = refs[:n_in], refs[n_in:]
    for n, scale, rate in plan:
        sums, (x_ref, m_ref, v_ref), ins = ins[:n], ins[n : n + 3], ins[n + 3 :]
        (x_out, m_out, v_out), outs = outs[:3], outs[3:]
        g = sums[0][...]
        for part in sums[1:]:
            g = g + part[...].astype(F32)
        x_out[...], m_out[...], v_out[...] = adam_update(
            x_ref[...], m_ref[...], v_ref[...], g * scale, rate
        )


def adam(*factors):
    plan = [(len(sums), scale, rate) for sums, _, scale, rate in factors]
    operands = [x for sums, state, _, _ in factors for x in (*sums, *state)]
    outs = [jax.ShapeDtypeStruct(x.shape, F32) for _, state, _, _ in factors for x in state]
    return pl.pallas_call(
        functools.partial(adam_kernel, plan),
        out_shape=outs,
        compiler_params=pltpu.CompilerParams(vmem_limit_bytes=SMALL_VMEM),
        name="adam",
    )(*operands)


def shards(response, difficulty, ability, ability_m, ability_v, discrim, discrim_m, discrim_v):
    n_item, n_mp = lax.axis_size("item"), lax.axis_size("mp")
    chips = n_item // 2
    rows, cols = response.shape
    k = discrim.shape[1] * n_mp
    items_total, ckpts_total = cols * n_item, rows * n_mp
    a_t, d_t = ability.T, discrim.T

    def send_chip(x, mask):
        return lax.ppermute(x, "item", swap_item(n_item, 2 * mask))

    def send_core(x):
        return lax.ppermute(x, "item", swap_item(n_item, 1))

    def send_mp(x, masks):
        return lax.ppermute(x, ("mp", "item"), swap_mp(n_mp, n_item, *masks))

    a_bf, d_bf = prepare(a_t, d_t)
    d_blocks = gather(d_bf, mp_basis(n_mp), send_mp)
    mine = [a_bf]
    for b in chip_basis(chips):
        mine += [send_chip(x, b) for x in mine]
        if len(mine) == 2 and n_mp > 2:
            mine[1], d_blocks[2] = lax.optimization_barrier((mine[1], d_blocks[2]))
    theirs = [send_core(x) for x in mine]
    theirs[0], difficulty = lax.optimization_barrier((theirs[0], difficulty))
    bias = (0.5 * difficulty).reshape(1, cols)
    keep, give, *h = gradients(mine + theirs, d_blocks, bias, response, n_mp, n_item)

    h_terms = [h[0]] + [send_mp(h[x], (x, x)) for x in range(1, n_mp)]
    g = pair_sum(keep, send_core(give), chips)
    g_terms = [g[0]] + [send_chip(g[x], x) for x in range(1, chips)]
    a_state = (a_t, ability_m.T, ability_v.T)
    d_state = (d_t, discrim_m.T, discrim_v.T)
    out = adam(
        (g_terms, a_state, 0.5 * math.sqrt(k / items_total), 0.05),
        (h_terms, d_state, 0.5 * math.sqrt(1.0 / ckpts_total), 0.01),
    )
    return tuple(x.T for x in out)


def solution(mesh):
    a_spec, d_spec = P("mp", "item"), P("item", "mp")
    return jax.shard_map(
        shards,
        mesh=mesh,
        in_specs=(a_spec, P("item")) + (a_spec,) * 3 + (d_spec,) * 3,
        out_specs=(a_spec,) * 3 + (d_spec,) * 3,
        check_vma=False,
    )
```

```python
import functools
import math

import jax
import jax.numpy as jnp
from jax import lax
from jax.experimental import pallas as pl
from jax.experimental.pallas import tpu as pltpu
from jax.sharding import PartitionSpec as P

beta_one = 0.9
beta_two = 0.999
corr_one = 1.0 - 0.9**10
corr_two = 1.0 - 0.999**10
adam_eps = 1e-08

BF = jnp.bfloat16
F32 = jnp.float32
VMEM_BYTES = 26 * 2**20
SMALL_VMEM = 8 * 2**20
ROW_TILE = 1024
COL_TILE = 512


def adam_update(factor, moment, second, gradient, step_rate):
    moment_new = beta_one * moment + (1.0 - beta_one) * gradient
    second_new = beta_two * second + (1.0 - beta_two) * gradient * gradient
    update = moment_new / corr_one / (jnp.sqrt(second_new / corr_two) + adam_eps)
    return (factor - step_rate * update, moment_new, second_new)


def prepare_kernel(a_ref, d_ref, a_out, d_out):
    a_out[...] = a_ref[...].astype(BF)
    d_out[...] = d_ref[...].astype(BF)


def prepare(a, d):
    shape = jax.ShapeDtypeStruct
    return pl.pallas_call(
        prepare_kernel,
        out_shape=(shape(a.shape, BF), shape(d.shape, BF)),
        compiler_params=pltpu.CompilerParams(vmem_limit_bytes=SMALL_VMEM),
        cost_estimate=pl.CostEstimate(flops=12000000000, bytes_accessed=8 * a.size, transcendentals=0),
        name="prepare",
    )(a, d)


def swap_item(n_item, mask):
    return [(i, i ^ mask) for i in range(n_item)]


def swap_mp(n_mp, n_item, even, odd):
    return [
        (m * n_item + i, (m ^ (odd if i % 2 else even)) * n_item + i)
        for m in range(n_mp)
        for i in range(n_item)
    ]


def chip_basis(chips):
    return [2**j - 1 for j in range(chips.bit_length() - 1, 0, -1)]


def mp_basis(n_mp):
    bits = [2**j for j in range(n_mp.bit_length() - 1)]
    return list(zip(bits, bits[1::-1] + bits[2:]))


def span(basis):
    masks = [0] if not basis or isinstance(basis[0], int) else [(0, 0)]
    for b in basis:
        if isinstance(b, int):
            masks += [x ^ b for x in masks]
        else:
            masks += [(x ^ b[0], y ^ b[1]) for x, y in masks]
    return masks


def gather(block, basis, send):
    blocks = [block]
    for b in basis:
        blocks += [send(x, b) for x in blocks]
    return blocks


def place_kernel(n_item, *refs):
    blocks, (at_ref, half_ref) = refs[:n_item], refs[n_item:]
    chips = n_item // 2
    ka = blocks[0].shape[0]
    item = lax.axis_index("item")
    chip, core = item // 2, lax.rem(item, 2)
    for q, (other, x) in enumerate((f, x) for f in range(2) for x in span(chip_basis(chips))):
        owner = (chip ^ x) * 2 + (core ^ other)
        at_ref[pl.ds(pl.multiple_of(owner * ka, ka), ka), :] = blocks[q][...]
    half_ref[...] = (at_ref[...].astype(F32) * 0.5).T.astype(BF)


def place_ability(blocks, n_item):
    k, rows = blocks[0].shape[0] * n_item, blocks[0].shape[1]
    return pl.pallas_call(
        functools.partial(place_kernel, n_item),
        out_shape=[jax.ShapeDtypeStruct((k, rows), BF), jax.ShapeDtypeStruct((rows, k), BF)],
        compiler_params=pltpu.CompilerParams(vmem_limit_bytes=SMALL_VMEM),
        name="place_ability",
    )(*blocks)


def grad_kernel(n_mp, n_item, *refs):
    chips = n_item // 2
    at, half, *d_in = refs[: 2 + n_mp]
    bias_ref, resp, keep_ref, give_ref, *h_out = refs[2 + n_mp : 6 + 2 * n_mp]
    dt, rs, gs, acc = refs[6 + 2 * n_mp :]
    k, rows = at.shape
    cols = dt.shape[1]
    ka, kd = k // n_item, k // n_mp

    item = lax.axis_index("item")
    m = lax.axis_index("mp")
    chip, core = item // 2, lax.rem(item, 2)

    def owner_item(x, flip):
        return (chip ^ x) * 2 + (core ^ flip)

    for q, (even, odd) in enumerate(span(mp_basis(n_mp))):
        off = pl.multiple_of((m ^ jnp.where(core == 0, even, odd)) * kd, kd)
        dt[pl.ds(off, kd), :] = d_in[q][...]
    acc[...] = jnp.zeros_like(acc)

    def step(t, carry):
        rng = pl.ds(pl.multiple_of(t * ROW_TILE, ROW_TILE), ROW_TILE)
        for c in range(0, cols, COL_TILE):
            cr = slice(c, c + COL_TILE)
            lg = jnp.dot(half[rng, :], dt[:, cr], preferred_element_type=F32) + bias_ref[:, cr]
            r = resp[rng, cr]
            sign = jnp.where(r == 2, -1.0, 1.0)
            rs[:, cr] = jnp.where(r == 0, 0.0, jnp.tanh(lg) + sign).astype(BF)
        gs[:, rng] = lax.dot_general(
            rs[...], dt[...], (((1,), (1,)), ((), ())), preferred_element_type=F32
        ).T
        for c in range(0, cols, COL_TILE):
            cr = slice(c, c + COL_TILE)
            acc[:, cr] += jnp.dot(at[:, rng], rs[:, cr], preferred_element_type=F32)
        return carry

    lax.fori_loop(0, rows // ROW_TILE, step, 0)

    for x in range(chips):
        dst = pl.ds(x * ka, ka)
        keep_ref[dst, :] = gs[pl.ds(pl.multiple_of(owner_item(x, 0) * ka, ka), ka), :]
        give_ref[dst, :] = gs[pl.ds(pl.multiple_of(owner_item(x, 1) * ka, ka), ka), :].astype(BF)
    for x in range(n_mp):
        h = acc[pl.ds(pl.multiple_of((m ^ x) * kd, kd), kd), :]
        h_out[x][...] = h.astype(h_out[x].dtype)


def gradients(at, half, d_blocks, bias, response, n_mp, n_item):
    k, rows = at.shape
    kd, cols = d_blocks[0].shape
    flops = 3 * 2 * rows * cols * k
    shape = jax.ShapeDtypeStruct
    vmem = pl.BlockSpec(memory_space=pltpu.VMEM)
    outs = [shape((k // 2, rows), F32), shape((k // 2, rows), BF)]
    outs += [shape((kd, cols), BF if q else F32) for q in range(n_mp)]
    return pl.pallas_call(
        functools.partial(grad_kernel, n_mp, n_item),
        out_shape=outs,
        in_specs=[vmem] * (4 + n_mp),
        out_specs=[vmem] * len(outs),
        scratch_shapes=[
            pltpu.VMEM((k, cols), BF),
            pltpu.VMEM((ROW_TILE, cols), BF),
            pltpu.VMEM((k, rows), F32),
            pltpu.VMEM((k, cols), F32),
        ],
        compiler_params=pltpu.CompilerParams(vmem_limit_bytes=VMEM_BYTES),
        cost_estimate=pl.CostEstimate(
            flops=flops, bytes_accessed=4 * rows * cols, transcendentals=rows * cols
        ),
        name="residual_gradients",
    )(at, half, *d_blocks, bias, response)


def pair_kernel(keep_ref, got_ref, *outs):
    ka = outs[0].shape[0]
    for x, out in enumerate(outs):
        rng = slice(x * ka, (x + 1) * ka)
        out[...] = (keep_ref[rng, :] + got_ref[rng, :].astype(F32)).astype(out.dtype)


def pair_sum(keep, got, chips):
    shape = (keep.shape[0] // chips, keep.shape[1])
    return pl.pallas_call(
        pair_kernel,
        out_shape=[jax.ShapeDtypeStruct(shape, BF if x else F32) for x in range(chips)],
        compiler_params=pltpu.CompilerParams(vmem_limit_bytes=SMALL_VMEM),
        name="core_pair_sum",
    )(keep, got)


def adam_kernel(plan, *refs):
    n_in = sum(n for n, _, _ in plan) + 3 * len(plan)
    ins, outs = refs[:n_in], refs[n_in:]
    for n, scale, rate in plan:
        sums, (x_ref, m_ref, v_ref), ins = ins[:n], ins[n : n + 3], ins[n + 3 :]
        (x_out, m_out, v_out), outs = outs[:3], outs[3:]
        g = sums[0][...]
        for part in sums[1:]:
            g = g + part[...].astype(F32)
        x_out[...], m_out[...], v_out[...] = adam_update(
            x_ref[...], m_ref[...], v_ref[...], g * scale, rate
        )


def adam(*factors):
    plan = [(len(sums), scale, rate) for sums, _, scale, rate in factors]
    operands = [x for sums, state, _, _ in factors for x in (*sums, *state)]
    outs = [jax.ShapeDtypeStruct(x.shape, F32) for _, state, _, _ in factors for x in state]
    return pl.pallas_call(
        functools.partial(adam_kernel, plan),
        out_shape=outs,
        compiler_params=pltpu.CompilerParams(vmem_limit_bytes=SMALL_VMEM),
        name="adam",
    )(*operands)


def shards(response, difficulty, ability, ability_m, ability_v, discrim, discrim_m, discrim_v):
    n_item, n_mp = lax.axis_size("item"), lax.axis_size("mp")
    chips = n_item // 2
    rows, cols = response.shape
    k = discrim.shape[1] * n_mp
    items_total, ckpts_total = cols * n_item, rows * n_mp
    a_t, d_t = ability.T, discrim.T

    def send_chip(x, mask):
        return lax.ppermute(x, "item", swap_item(n_item, 2 * mask))

    def send_core(x):
        return lax.ppermute(x, "item", swap_item(n_item, 1))

    def send_mp(x, masks):
        return lax.ppermute(x, ("mp", "item"), swap_mp(n_mp, n_item, *masks))

    a_bf, d_bf = prepare(a_t, d_t)
    d_blocks = gather(d_bf, mp_basis(n_mp), send_mp)
    mine = [a_bf]
    for b in chip_basis(chips):
        mine += [send_chip(x, b) for x in mine]
        if len(mine) == 2 and n_mp > 2:
            mine[1], d_blocks[2] = lax.optimization_barrier((mine[1], d_blocks[2]))
    theirs = [send_core(x) for x in mine]
    theirs[0], difficulty = lax.optimization_barrier((theirs[0], difficulty))
    bias = (0.5 * difficulty).reshape(1, cols)
    at, half = place_ability(mine + theirs, n_item)
    keep, give, *h = gradients(at, half, d_blocks, bias, response, n_mp, n_item)

    h_terms = [h[0]] + [send_mp(h[x], (x, x)) for x in range(1, n_mp)]
    g = pair_sum(keep, send_core(give), chips)
    g_terms = [g[0]] + [send_chip(g[x], x) for x in range(1, chips)]
    a_state = (a_t, ability_m.T, ability_v.T)
    d_state = (d_t, discrim_m.T, discrim_v.T)
    d_out = list(adam((h_terms, d_state, 0.5 * math.sqrt(1.0 / ckpts_total), 0.01)))
    g_terms[0], d_out[0] = lax.optimization_barrier((g_terms[0], d_out[0]))
    a_out = adam((g_terms, a_state, 0.5 * math.sqrt(k / items_total), 0.05))
    out = (*a_out, *d_out)
    return tuple(x.T for x in out)


def solution(mesh):
    a_spec, d_spec = P("mp", "item"), P("item", "mp")
    return jax.shard_map(
        shards,
        mesh=mesh,
        in_specs=(a_spec, P("item")) + (a_spec,) * 3 + (d_spec,) * 3,
        out_specs=(a_spec,) * 3 + (d_spec,) * 3,
        check_vma=False,
    )
```

```python
import functools
import math

import jax
import jax.numpy as jnp
from jax import lax
from jax.experimental import pallas as pl
from jax.experimental.pallas import tpu as pltpu
from jax.sharding import PartitionSpec as P

beta_one = 0.9
beta_two = 0.999
corr_one = 1.0 - 0.9**10
corr_two = 1.0 - 0.999**10
adam_eps = 1e-08

BF = jnp.bfloat16
F32 = jnp.float32
VMEM_BYTES = 26 * 2**20
SMALL_VMEM = 8 * 2**20
ROW_TILE = 1024
COL_TILE = 512


def adam_update(factor, moment, second, gradient, step_rate):
    moment_new = beta_one * moment + (1.0 - beta_one) * gradient
    second_new = beta_two * second + (1.0 - beta_two) * gradient * gradient
    update = moment_new / corr_one / (jnp.sqrt(second_new / corr_two) + adam_eps)
    return (factor - step_rate * update, moment_new, second_new)


def ones_kernel(out_ref):
    out_ref[...] = jnp.ones_like(out_ref)


def ones_first():
    return pl.pallas_call(
        ones_kernel,
        out_shape=jax.ShapeDtypeStruct((8, 128), F32),
        compiler_params=pltpu.CompilerParams(vmem_limit_bytes=SMALL_VMEM),
        cost_estimate=pl.CostEstimate(flops=12000000000, bytes_accessed=4096, transcendentals=0),
        name="ones_first",
    )()


def prepare_kernel(one_ref, a_ref, d_ref, a_out, d_out):
    one = one_ref[0:1, 0:1]
    a_out[...] = (a_ref[...] * one).astype(BF)
    d_out[...] = (d_ref[...] * one).astype(BF)


def prepare(a, d):
    shape = jax.ShapeDtypeStruct
    return pl.pallas_call(
        prepare_kernel,
        out_shape=(shape(a.shape, BF), shape(d.shape, BF)),
        compiler_params=pltpu.CompilerParams(vmem_limit_bytes=SMALL_VMEM),
        cost_estimate=pl.CostEstimate(
            flops=1000000, bytes_accessed=8 * a.size, transcendentals=0
        ),
        name="prepare",
    )(ones_first(), a, d)


def swap_item(n_item, mask):
    return [(i, i ^ mask) for i in range(n_item)]


def swap_mp(n_mp, n_item, even, odd):
    return [
        (m * n_item + i, (m ^ (odd if i % 2 else even)) * n_item + i)
        for m in range(n_mp)
        for i in range(n_item)
    ]


def chip_basis(chips):
    return [2**j - 1 for j in range(chips.bit_length() - 1, 0, -1)]


def mp_basis(n_mp):
    bits = [2**j for j in range(n_mp.bit_length() - 1)]
    return list(zip(bits, bits[1::-1] + bits[2:]))


def span(basis):
    masks = [0] if not basis or isinstance(basis[0], int) else [(0, 0)]
    for b in basis:
        if isinstance(b, int):
            masks += [x ^ b for x in masks]
        else:
            masks += [(x ^ b[0], y ^ b[1]) for x, y in masks]
    return masks


def gather(block, basis, send):
    blocks = [block]
    for b in basis:
        blocks += [send(x, b) for x in blocks]
    return blocks


def place_kernel(n_item, *refs):
    blocks, (at_ref, half_ref) = refs[:n_item], refs[n_item:]
    chips = n_item // 2
    ka = blocks[0].shape[0]
    item = lax.axis_index("item")
    chip, core = item // 2, lax.rem(item, 2)
    for q, (other, x) in enumerate((f, x) for f in range(2) for x in span(chip_basis(chips))):
        owner = (chip ^ x) * 2 + (core ^ other)
        at_ref[pl.ds(pl.multiple_of(owner * ka, ka), ka), :] = blocks[q][...]
    half_ref[...] = (at_ref[...].astype(F32) * 0.5).T.astype(BF)


def place_ability(blocks, n_item):
    k, rows = blocks[0].shape[0] * n_item, blocks[0].shape[1]
    return pl.pallas_call(
        functools.partial(place_kernel, n_item),
        out_shape=[jax.ShapeDtypeStruct((k, rows), BF), jax.ShapeDtypeStruct((rows, k), BF)],
        compiler_params=pltpu.CompilerParams(vmem_limit_bytes=SMALL_VMEM),
        name="place_ability",
    )(*blocks)


def ability_kernel(n_mp, n_item, *refs):
    chips = n_item // 2
    half, *d_in = refs[: 1 + n_mp]
    bias_ref, resp, res_ref, keep_ref, give_ref, dt, gs = refs[1 + n_mp :]
    rows, k = half.shape
    cols = dt.shape[1]
    ka, kd = k // n_item, k // n_mp

    item = lax.axis_index("item")
    m = lax.axis_index("mp")
    chip, core = item // 2, lax.rem(item, 2)

    def owner_item(x, flip):
        return (chip ^ x) * 2 + (core ^ flip)

    for q, (even, odd) in enumerate(span(mp_basis(n_mp))):
        off = pl.multiple_of((m ^ jnp.where(core == 0, even, odd)) * kd, kd)
        dt[pl.ds(off, kd), :] = d_in[q][...]

    def step(t, carry):
        rng = pl.ds(pl.multiple_of(t * ROW_TILE, ROW_TILE), ROW_TILE)
        for c in range(0, cols, COL_TILE):
            cr = slice(c, c + COL_TILE)
            lg = jnp.dot(half[rng, :], dt[:, cr], preferred_element_type=F32) + bias_ref[:, cr]
            r = resp[rng, cr]
            sign = jnp.where(r == 2, -1.0, 1.0)
            res_ref[rng, cr] = jnp.where(r == 0, 0.0, jnp.tanh(lg) + sign).astype(BF)
        gs[:, rng] = lax.dot_general(
            res_ref[rng, :], dt[...], (((1,), (1,)), ((), ())), preferred_element_type=F32
        ).T
        return carry

    lax.fori_loop(0, rows // ROW_TILE, step, 0)

    for x in range(chips):
        dst = pl.ds(x * ka, ka)
        keep_ref[dst, :] = gs[pl.ds(pl.multiple_of(owner_item(x, 0) * ka, ka), ka), :]
        give_ref[dst, :] = gs[pl.ds(pl.multiple_of(owner_item(x, 1) * ka, ka), ka), :].astype(BF)


def ability_gradient(half, d_blocks, bias, response, n_mp, n_item):
    rows, k = half.shape
    cols = response.shape[1]
    shape = jax.ShapeDtypeStruct
    vmem = pl.BlockSpec(memory_space=pltpu.VMEM)
    return pl.pallas_call(
        functools.partial(ability_kernel, n_mp, n_item),
        out_shape=[shape((rows, cols), BF), shape((k // 2, rows), F32), shape((k // 2, rows), BF)],
        in_specs=[vmem] * (3 + n_mp),
        out_specs=[vmem] * 3,
        scratch_shapes=[pltpu.VMEM((k, cols), BF), pltpu.VMEM((k, rows), F32)],
        compiler_params=pltpu.CompilerParams(vmem_limit_bytes=VMEM_BYTES),
        cost_estimate=pl.CostEstimate(
            flops=2 * 2 * rows * cols * k, bytes_accessed=4 * rows * cols, transcendentals=rows * cols
        ),
        name="residual_ability_gradient",
    )(half, *d_blocks, bias, response)


def discrim_kernel(n_mp, at, res, *refs):
    h_out, acc = refs[:n_mp], refs[n_mp]
    kd, cols = h_out[0].shape
    m = lax.axis_index("mp")
    for c in range(0, cols, COL_TILE):
        cr = slice(c, c + COL_TILE)
        acc[:, cr] = jnp.dot(at[...], res[:, cr], preferred_element_type=F32)
    for x in range(n_mp):
        h = acc[pl.ds(pl.multiple_of((m ^ x) * kd, kd), kd), :]
        h_out[x][...] = h.astype(h_out[x].dtype)


def discrim_gradient(at, res, n_mp):
    k, rows = at.shape
    cols = res.shape[1]
    shape = jax.ShapeDtypeStruct
    vmem = pl.BlockSpec(memory_space=pltpu.VMEM)
    return pl.pallas_call(
        functools.partial(discrim_kernel, n_mp),
        out_shape=[shape((k // n_mp, cols), BF if q else F32) for q in range(n_mp)],
        in_specs=[vmem] * 2,
        out_specs=[vmem] * n_mp,
        scratch_shapes=[pltpu.VMEM((k, cols), F32)],
        compiler_params=pltpu.CompilerParams(vmem_limit_bytes=SMALL_VMEM * 2),
        cost_estimate=pl.CostEstimate(
            flops=2 * rows * cols * k, bytes_accessed=2 * rows * cols, transcendentals=0
        ),
        name="discrim_gradient",
    )(at, res)


def pair_kernel(keep_ref, got_ref, *outs):
    ka = outs[0].shape[0]
    for x, out in enumerate(outs):
        rng = slice(x * ka, (x + 1) * ka)
        out[...] = (keep_ref[rng, :] + got_ref[rng, :].astype(F32)).astype(out.dtype)


def pair_sum(keep, got, kinds):
    shape = (keep.shape[0] // len(kinds), keep.shape[1])
    return pl.pallas_call(
        pair_kernel,
        out_shape=[jax.ShapeDtypeStruct(shape, kind) for kind in kinds],
        compiler_params=pltpu.CompilerParams(vmem_limit_bytes=SMALL_VMEM),
        name="core_pair_sum",
    )(keep, got)


def add_kernel(x_ref, y_ref, out_ref):
    out_ref[...] = (x_ref[...] + y_ref[...].astype(F32)).astype(BF)


def add(x, y):
    return pl.pallas_call(
        add_kernel,
        out_shape=jax.ShapeDtypeStruct(x.shape, BF),
        compiler_params=pltpu.CompilerParams(vmem_limit_bytes=SMALL_VMEM),
        cost_estimate=pl.CostEstimate(flops=4000000000, bytes_accessed=8 * x.size, transcendentals=0),
        name="add_partial",
    )(x, y)


def adam_kernel(plan, *refs):
    n_in = sum(n for n, _, _ in plan) + 3 * len(plan)
    ins, outs = refs[:n_in], refs[n_in:]
    for n, scale, rate in plan:
        sums, (x_ref, m_ref, v_ref), ins = ins[:n], ins[n : n + 3], ins[n + 3 :]
        (x_out, m_out, v_out), outs = outs[:3], outs[3:]
        g = sums[0][...]
        for part in sums[1:]:
            g = g + part[...].astype(F32)
        x_out[...], m_out[...], v_out[...] = adam_update(
            x_ref[...], m_ref[...], v_ref[...], g * scale, rate
        )


def adam(*factors):
    plan = [(len(sums), scale, rate) for sums, _, scale, rate in factors]
    operands = [x for sums, state, _, _ in factors for x in (*sums, *state)]
    outs = [jax.ShapeDtypeStruct(x.shape, F32) for _, state, _, _ in factors for x in state]
    return pl.pallas_call(
        functools.partial(adam_kernel, plan),
        out_shape=outs,
        compiler_params=pltpu.CompilerParams(vmem_limit_bytes=SMALL_VMEM),
        name="adam",
    )(*operands)


def shards(response, difficulty, ability, ability_m, ability_v, discrim, discrim_m, discrim_v):
    n_item, n_mp = lax.axis_size("item"), lax.axis_size("mp")
    chips = n_item // 2
    rows, cols = response.shape
    k = discrim.shape[1] * n_mp
    items_total, ckpts_total = cols * n_item, rows * n_mp
    a_t, d_t = ability.T, discrim.T

    def send_chip(x, mask):
        return lax.ppermute(x, "item", swap_item(n_item, 2 * mask))

    def send_core(x):
        return lax.ppermute(x, "item", swap_item(n_item, 1))

    def send_mp(x, masks):
        return lax.ppermute(x, ("mp", "item"), swap_mp(n_mp, n_item, *masks))

    a_bf, d_bf = prepare(a_t, d_t)
    d_blocks = gather(d_bf, mp_basis(n_mp), send_mp)
    mine = [a_bf]
    for b in chip_basis(chips):
        mine += [send_chip(x, b) for x in mine]
        if len(mine) == 2 and n_mp > 2:
            mine[1], d_blocks[2] = lax.optimization_barrier((mine[1], d_blocks[2]))
    theirs = [send_core(x) for x in mine]
    theirs[0], difficulty = lax.optimization_barrier((theirs[0], difficulty))
    bias = (0.5 * difficulty).reshape(1, cols)
    at, half = place_ability(mine + theirs, n_item)
    res, keep, give = ability_gradient(half, d_blocks, bias, response, n_mp, n_item)
    got = send_core(give)
    h = list(discrim_gradient(at, res, n_mp))

    via = [x for x in range(3, chips, 2)]
    got, h[0] = lax.optimization_barrier((got, h[0]))
    g = list(pair_sum(keep, got, [F32 if x == 0 or x ^ 1 in via else BF for x in range(chips)]))
    for x in via:
        g[x ^ 1] = add(g[x ^ 1], send_chip(g[x], 1))
    if via:
        last = max(via) ^ 1
        g[1], g[last] = lax.optimization_barrier((g[1], g[last]))
    h_terms = [h[0]] + [send_mp(h[x], (x, x)) for x in range(1, n_mp)]
    g_terms = [g[0]] + [send_chip(g[x], x) for x in range(chips - 1, 0, -1) if x not in via]
    a_state = (a_t, ability_m.T, ability_v.T)
    d_state = (d_t, discrim_m.T, discrim_v.T)
    d_out = list(adam((h_terms, d_state, 0.5 * math.sqrt(1.0 / ckpts_total), 0.01)))
    g_terms[0], d_out[0] = lax.optimization_barrier((g_terms[0], d_out[0]))
    a_out = adam((g_terms, a_state, 0.5 * math.sqrt(k / items_total), 0.05))
    out = (*a_out, *d_out)
    return tuple(x.T for x in out)


def solution(mesh):
    a_spec, d_spec = P("mp", "item"), P("item", "mp")
    return jax.shard_map(
        shards,
        mesh=mesh,
        in_specs=(a_spec, P("item")) + (a_spec,) * 3 + (d_spec,) * 3,
        out_specs=(a_spec,) * 3 + (d_spec,) * 3,
        check_vma=False,
    )
```

```python
import functools
import math

import jax
import jax.numpy as jnp
from jax import lax
from jax.experimental import pallas as pl
from jax.experimental.pallas import tpu as pltpu
from jax.sharding import PartitionSpec as P

beta_one = 0.9
beta_two = 0.999
corr_one = 1.0 - 0.9**10
corr_two = 1.0 - 0.999**10
adam_eps = 1e-08

BF = jnp.bfloat16
F32 = jnp.float32
VMEM_BYTES = 26 * 2**20
SMALL_VMEM = 8 * 2**20
ROW_TILE = 1024
COL_TILE = 512


def adam_update(factor, moment, second, gradient, step_rate):
    moment_new = beta_one * moment + (1.0 - beta_one) * gradient
    second_new = beta_two * second + (1.0 - beta_two) * gradient * gradient
    update = moment_new / corr_one / (jnp.sqrt(second_new / corr_two) + adam_eps)
    return (factor - step_rate * update, moment_new, second_new)


def ones_kernel(out_ref):
    out_ref[...] = jnp.ones_like(out_ref)


def ones_first():
    return pl.pallas_call(
        ones_kernel,
        out_shape=jax.ShapeDtypeStruct((8, 128), F32),
        compiler_params=pltpu.CompilerParams(vmem_limit_bytes=SMALL_VMEM),
        cost_estimate=pl.CostEstimate(flops=12000000000, bytes_accessed=4096, transcendentals=0),
        name="ones_first",
    )()


def prepare_kernel(one_ref, a_ref, d_ref, a_out, d_out):
    one = one_ref[0:1, 0:1]
    a_out[...] = (a_ref[...] * one).astype(BF)
    d_out[...] = (d_ref[...] * one).astype(BF)


def prepare(a, d):
    shape = jax.ShapeDtypeStruct
    return pl.pallas_call(
        prepare_kernel,
        out_shape=(shape(a.shape, BF), shape(d.shape, BF)),
        compiler_params=pltpu.CompilerParams(vmem_limit_bytes=SMALL_VMEM),
        cost_estimate=pl.CostEstimate(
            flops=1000000, bytes_accessed=8 * a.size, transcendentals=0
        ),
        name="prepare",
    )(ones_first(), a, d)


def swap_item(n_item, mask):
    return [(i, i ^ mask) for i in range(n_item)]


def swap_mp(n_mp, n_item, even, odd):
    return [
        (m * n_item + i, (m ^ (odd if i % 2 else even)) * n_item + i)
        for m in range(n_mp)
        for i in range(n_item)
    ]


def chip_basis(chips):
    return [2**j - 1 for j in range(chips.bit_length() - 1, 0, -1)]


def mp_basis(n_mp):
    bits = [2**j for j in range(n_mp.bit_length() - 1)]
    return list(zip(bits, bits[1::-1] + bits[2:]))


def span(basis):
    masks = [0] if not basis or isinstance(basis[0], int) else [(0, 0)]
    for b in basis:
        if isinstance(b, int):
            masks += [x ^ b for x in masks]
        else:
            masks += [(x ^ b[0], y ^ b[1]) for x, y in masks]
    return masks


def gather(block, basis, send):
    blocks = [block]
    for b in basis:
        blocks += [send(x, b) for x in blocks]
    return blocks


def place_kernel(n_item, *refs):
    blocks, (at_ref, half_ref) = refs[:n_item], refs[n_item:]
    chips = n_item // 2
    ka = blocks[0].shape[0]
    item = lax.axis_index("item")
    chip, core = item // 2, lax.rem(item, 2)
    for q, (other, x) in enumerate((f, x) for f in range(2) for x in span(chip_basis(chips))):
        owner = (chip ^ x) * 2 + (core ^ other)
        at_ref[pl.ds(pl.multiple_of(owner * ka, ka), ka), :] = blocks[q][...]
    half_ref[...] = (at_ref[...].astype(F32) * 0.5).T.astype(BF)


def place_ability(blocks, n_item):
    k, rows = blocks[0].shape[0] * n_item, blocks[0].shape[1]
    return pl.pallas_call(
        functools.partial(place_kernel, n_item),
        out_shape=[jax.ShapeDtypeStruct((k, rows), BF), jax.ShapeDtypeStruct((rows, k), BF)],
        compiler_params=pltpu.CompilerParams(vmem_limit_bytes=SMALL_VMEM),
        name="place_ability",
    )(*blocks)


def ability_kernel(n_mp, n_item, *refs):
    chips = n_item // 2
    half, *d_in = refs[: 1 + n_mp]
    bias_ref, resp, res_ref, keep_ref, give_ref, dt, gs = refs[1 + n_mp :]
    rows, k = half.shape
    cols = dt.shape[1]
    ka, kd = k // n_item, k // n_mp

    item = lax.axis_index("item")
    m = lax.axis_index("mp")
    chip, core = item // 2, lax.rem(item, 2)

    def owner_item(x, flip):
        return (chip ^ x) * 2 + (core ^ flip)

    for q, (even, odd) in enumerate(span(mp_basis(n_mp))):
        off = pl.multiple_of((m ^ jnp.where(core == 0, even, odd)) * kd, kd)
        dt[pl.ds(off, kd), :] = d_in[q][...]

    def step(t, carry):
        rng = pl.ds(t * ROW_TILE, ROW_TILE)
        for c in range(0, cols, COL_TILE):
            cr = slice(c, c + COL_TILE)
            lg = jnp.dot(half[rng, :], dt[:, cr], preferred_element_type=F32) + bias_ref[:, cr]
            r = resp[rng, cr]
            sign = jnp.where(r == 2, -1.0, 1.0)
            res_ref[rng, cr] = jnp.where(r == 0, 0.0, jnp.tanh(lg) + sign).astype(BF)
        gs[:, rng] = lax.dot_general(
            res_ref[rng, :], dt[...], (((1,), (1,)), ((), ())), preferred_element_type=F32
        ).T
        return carry

    for t in range(rows // ROW_TILE):
        step(t, 0)

    for x in range(chips):
        dst = pl.ds(x * ka, ka)
        keep_ref[dst, :] = gs[pl.ds(pl.multiple_of(owner_item(x, 0) * ka, ka), ka), :]
        give_ref[dst, :] = gs[pl.ds(pl.multiple_of(owner_item(x, 1) * ka, ka), ka), :].astype(BF)


def ability_gradient(half, d_blocks, bias, response, n_mp, n_item):
    rows, k = half.shape
    cols = response.shape[1]
    shape = jax.ShapeDtypeStruct
    vmem = pl.BlockSpec(memory_space=pltpu.VMEM)
    return pl.pallas_call(
        functools.partial(ability_kernel, n_mp, n_item),
        out_shape=[shape((rows, cols), BF), shape((k // 2, rows), F32), shape((k // 2, rows), BF)],
        in_specs=[vmem] * (3 + n_mp),
        out_specs=[vmem] * 3,
        scratch_shapes=[pltpu.VMEM((k, cols), BF), pltpu.VMEM((k, rows), F32)],
        compiler_params=pltpu.CompilerParams(vmem_limit_bytes=VMEM_BYTES),
        cost_estimate=pl.CostEstimate(
            flops=2 * 2 * rows * cols * k, bytes_accessed=4 * rows * cols, transcendentals=rows * cols
        ),
        name="residual_ability_gradient",
    )(half, *d_blocks, bias, response)


def discrim_kernel(n_mp, at, res, *refs):
    h_out, acc = refs[:n_mp], refs[n_mp]
    kd, cols = h_out[0].shape
    m = lax.axis_index("mp")
    for c in range(0, cols, COL_TILE):
        cr = slice(c, c + COL_TILE)
        acc[:, cr] = jnp.dot(at[...], res[:, cr], preferred_element_type=F32)
    for x in range(n_mp):
        h = acc[pl.ds(pl.multiple_of((m ^ x) * kd, kd), kd), :]
        h_out[x][...] = h.astype(h_out[x].dtype)


def discrim_gradient(at, res, n_mp):
    k, rows = at.shape
    cols = res.shape[1]
    shape = jax.ShapeDtypeStruct
    vmem = pl.BlockSpec(memory_space=pltpu.VMEM)
    return pl.pallas_call(
        functools.partial(discrim_kernel, n_mp),
        out_shape=[shape((k // n_mp, cols), BF if q else F32) for q in range(n_mp)],
        in_specs=[vmem] * 2,
        out_specs=[vmem] * n_mp,
        scratch_shapes=[pltpu.VMEM((k, cols), F32)],
        compiler_params=pltpu.CompilerParams(vmem_limit_bytes=SMALL_VMEM * 2),
        cost_estimate=pl.CostEstimate(
            flops=2 * rows * cols * k, bytes_accessed=2 * rows * cols, transcendentals=0
        ),
        name="discrim_gradient",
    )(at, res)


def pair_kernel(keep_ref, got_ref, *outs):
    ka = outs[0].shape[0]
    for x, out in enumerate(outs):
        rng = slice(x * ka, (x + 1) * ka)
        out[...] = (keep_ref[rng, :] + got_ref[rng, :].astype(F32)).astype(out.dtype)


def pair_sum(keep, got, kinds):
    shape = (keep.shape[0] // len(kinds), keep.shape[1])
    return pl.pallas_call(
        pair_kernel,
        out_shape=[jax.ShapeDtypeStruct(shape, kind) for kind in kinds],
        compiler_params=pltpu.CompilerParams(vmem_limit_bytes=SMALL_VMEM),
        name="core_pair_sum",
    )(keep, got)


def add_kernel(x_ref, y_ref, out_ref):
    out_ref[...] = (x_ref[...] + y_ref[...].astype(F32)).astype(BF)


def add(x, y):
    return pl.pallas_call(
        add_kernel,
        out_shape=jax.ShapeDtypeStruct(x.shape, BF),
        compiler_params=pltpu.CompilerParams(vmem_limit_bytes=SMALL_VMEM),
        cost_estimate=pl.CostEstimate(flops=4000000000, bytes_accessed=8 * x.size, transcendentals=0),
        name="add_partial",
    )(x, y)


def adam_kernel(plan, *refs):
    n_in = sum(n for n, _, _ in plan) + 3 * len(plan)
    ins, outs = refs[:n_in], refs[n_in:]
    for n, scale, rate in plan:
        sums, (x_ref, m_ref, v_ref), ins = ins[:n], ins[n : n + 3], ins[n + 3 :]
        (x_out, m_out, v_out), outs = outs[:3], outs[3:]
        g = sums[0][...]
        for part in sums[1:]:
            g = g + part[...].astype(F32)
        x_out[...], m_out[...], v_out[...] = adam_update(
            x_ref[...], m_ref[...], v_ref[...], g * scale, rate
        )


def adam(*factors):
    plan = [(len(sums), scale, rate) for sums, _, scale, rate in factors]
    operands = [x for sums, state, _, _ in factors for x in (*sums, *state)]
    outs = [jax.ShapeDtypeStruct(x.shape, F32) for _, state, _, _ in factors for x in state]
    return pl.pallas_call(
        functools.partial(adam_kernel, plan),
        out_shape=outs,
        compiler_params=pltpu.CompilerParams(vmem_limit_bytes=SMALL_VMEM),
        name="adam",
    )(*operands)


def shards(response, difficulty, ability, ability_m, ability_v, discrim, discrim_m, discrim_v):
    n_item, n_mp = lax.axis_size("item"), lax.axis_size("mp")
    chips = n_item // 2
    rows, cols = response.shape
    k = discrim.shape[1] * n_mp
    items_total, ckpts_total = cols * n_item, rows * n_mp
    a_t, d_t = ability.T, discrim.T

    def send_chip(x, mask):
        return lax.ppermute(x, "item", swap_item(n_item, 2 * mask))

    def send_core(x):
        return lax.ppermute(x, "item", swap_item(n_item, 1))

    def send_mp(x, masks):
        return lax.ppermute(x, ("mp", "item"), swap_mp(n_mp, n_item, *masks))

    a_bf, d_bf = prepare(a_t, d_t)
    d_blocks = gather(d_bf, mp_basis(n_mp), send_mp)
    mine = [a_bf]
    for b in chip_basis(chips):
        mine += [send_chip(x, b) for x in mine]
        if len(mine) == 2 and n_mp > 2:
            mine[1], d_blocks[2] = lax.optimization_barrier((mine[1], d_blocks[2]))
    theirs = [send_core(x) for x in mine]
    theirs[0], difficulty = lax.optimization_barrier((theirs[0], difficulty))
    bias = (0.5 * difficulty).reshape(1, cols)
    at, half = place_ability(mine + theirs, n_item)
    res, keep, give = ability_gradient(half, d_blocks, bias, response, n_mp, n_item)
    got = send_core(give)
    h = list(discrim_gradient(at, res, n_mp))

    via = [x for x in range(3, chips, 2)]
    got, h[0] = lax.optimization_barrier((got, h[0]))
    g = list(pair_sum(keep, got, [F32 if x == 0 or x ^ 1 in via else BF for x in range(chips)]))
    for x in via:
        g[x ^ 1] = add(g[x ^ 1], send_chip(g[x], 1))
    if via:
        last = max(via) ^ 1
        g[1], g[last] = lax.optimization_barrier((g[1], g[last]))
    h_terms = [h[0]] + [send_mp(h[x], (x, x)) for x in range(1, n_mp)]
    g_terms = [g[0]] + [send_chip(g[x], x) for x in range(chips - 1, 0, -1) if x not in via]
    a_state = (a_t, ability_m.T, ability_v.T)
    d_state = (d_t, discrim_m.T, discrim_v.T)
    d_out = list(adam((h_terms, d_state, 0.5 * math.sqrt(1.0 / ckpts_total), 0.01)))
    g_terms[0], d_out[0] = lax.optimization_barrier((g_terms[0], d_out[0]))
    a_out = adam((g_terms, a_state, 0.5 * math.sqrt(k / items_total), 0.05))
    out = (*a_out, *d_out)
    return tuple(x.T for x in out)


def solution(mesh):
    a_spec, d_spec = P("mp", "item"), P("item", "mp")
    return jax.shard_map(
        shards,
        mesh=mesh,
        in_specs=(a_spec, P("item")) + (a_spec,) * 3 + (d_spec,) * 3,
        out_specs=(a_spec,) * 3 + (d_spec,) * 3,
        check_vma=False,
    )
```

```python
import functools
import math

import jax
import jax.numpy as jnp
from jax import lax
from jax.experimental import pallas as pl
from jax.experimental.pallas import tpu as pltpu
from jax.sharding import PartitionSpec as P

beta_one = 0.9
beta_two = 0.999
corr_one = 1.0 - 0.9**10
corr_two = 1.0 - 0.999**10
adam_eps = 1e-08

BF = jnp.bfloat16
F32 = jnp.float32
VMEM_BYTES = 26 * 2**20
SMALL_VMEM = 8 * 2**20
ROW_TILE = 512
COL_TILE = 512


def adam_update(factor, moment, second, gradient, step_rate):
    moment_new = beta_one * moment + (1.0 - beta_one) * gradient
    second_new = beta_two * second + (1.0 - beta_two) * gradient * gradient
    update = moment_new / corr_one / (jnp.sqrt(second_new / corr_two) + adam_eps)
    return (factor - step_rate * update, moment_new, second_new)


def ones_kernel(out_ref):
    out_ref[...] = jnp.ones_like(out_ref)


def ones_first():
    return pl.pallas_call(
        ones_kernel,
        out_shape=jax.ShapeDtypeStruct((8, 128), F32),
        compiler_params=pltpu.CompilerParams(vmem_limit_bytes=SMALL_VMEM),
        cost_estimate=pl.CostEstimate(flops=12000000000, bytes_accessed=4096, transcendentals=0),
        name="ones_first",
    )()


def prepare_kernel(one_ref, a_ref, d_ref, a_out, d_out):
    one = one_ref[0:1, 0:1]
    a_out[...] = (a_ref[...] * one).astype(BF)
    d_out[...] = (d_ref[...] * one).astype(BF)


def prepare(a, d):
    shape = jax.ShapeDtypeStruct
    return pl.pallas_call(
        prepare_kernel,
        out_shape=(shape(a.shape, BF), shape(d.shape, BF)),
        compiler_params=pltpu.CompilerParams(vmem_limit_bytes=SMALL_VMEM),
        cost_estimate=pl.CostEstimate(
            flops=1000000, bytes_accessed=8 * a.size, transcendentals=0
        ),
        name="prepare",
    )(ones_first(), a, d)


def swap_item(n_item, mask):
    return [(i, i ^ mask) for i in range(n_item)]


def swap_mp(n_mp, n_item, even, odd):
    return [
        (m * n_item + i, (m ^ (odd if i % 2 else even)) * n_item + i)
        for m in range(n_mp)
        for i in range(n_item)
    ]


def chip_basis(chips):
    return [2**j - 1 for j in range(chips.bit_length() - 1, 0, -1)]


def mp_basis(n_mp):
    bits = [2**j for j in range(n_mp.bit_length() - 1)]
    return list(zip(bits, bits[1::-1] + bits[2:]))


def span(basis):
    masks = [0] if not basis or isinstance(basis[0], int) else [(0, 0)]
    for b in basis:
        if isinstance(b, int):
            masks += [x ^ b for x in masks]
        else:
            masks += [(x ^ b[0], y ^ b[1]) for x, y in masks]
    return masks


def gather(block, basis, send):
    blocks = [block]
    for b in basis:
        blocks += [send(x, b) for x in blocks]
    return blocks


def place_kernel(n_item, *refs):
    blocks, (at_ref, half_ref) = refs[:n_item], refs[n_item:]
    chips = n_item // 2
    ka = blocks[0].shape[0]
    item = lax.axis_index("item")
    chip, core = item // 2, lax.rem(item, 2)
    for q, (other, x) in enumerate((f, x) for f in range(2) for x in span(chip_basis(chips))):
        owner = (chip ^ x) * 2 + (core ^ other)
        at_ref[pl.ds(pl.multiple_of(owner * ka, ka), ka), :] = blocks[q][...]
    half_ref[...] = (at_ref[...].astype(F32) * 0.5).T.astype(BF)


def place_ability(blocks, n_item):
    k, rows = blocks[0].shape[0] * n_item, blocks[0].shape[1]
    return pl.pallas_call(
        functools.partial(place_kernel, n_item),
        out_shape=[jax.ShapeDtypeStruct((k, rows), BF), jax.ShapeDtypeStruct((rows, k), BF)],
        compiler_params=pltpu.CompilerParams(vmem_limit_bytes=SMALL_VMEM),
        name="place_ability",
    )(*blocks)


def ability_kernel(n_mp, n_item, *refs):
    chips = n_item // 2
    half, *d_in = refs[: 1 + n_mp]
    bias_ref, resp, res_ref, keep_ref, give_ref, dt, gs = refs[1 + n_mp :]
    rows, k = half.shape
    cols = dt.shape[1]
    ka, kd = k // n_item, k // n_mp

    item = lax.axis_index("item")
    m = lax.axis_index("mp")
    chip, core = item // 2, lax.rem(item, 2)

    def owner_item(x, flip):
        return (chip ^ x) * 2 + (core ^ flip)

    for q, (even, odd) in enumerate(span(mp_basis(n_mp))):
        off = pl.multiple_of((m ^ jnp.where(core == 0, even, odd)) * kd, kd)
        dt[pl.ds(off, kd), :] = d_in[q][...]

    def step(t, carry):
        rng = pl.ds(t * ROW_TILE, ROW_TILE)
        for c in range(0, cols, COL_TILE):
            cr = slice(c, c + COL_TILE)
            lg = jnp.dot(half[rng, :], dt[:, cr], preferred_element_type=F32) + bias_ref[:, cr]
            r = resp[rng, cr]
            sign = jnp.where(r == 2, -1.0, 1.0)
            res_ref[rng, cr] = jnp.where(r == 0, 0.0, jnp.tanh(lg) + sign).astype(BF)
        gs[:, rng] = lax.dot_general(
            res_ref[rng, :], dt[...], (((1,), (1,)), ((), ())), preferred_element_type=F32
        ).T
        return carry

    for t in range(rows // ROW_TILE):
        step(t, 0)

    for x in range(chips):
        dst = pl.ds(x * ka, ka)
        keep_ref[dst, :] = gs[pl.ds(pl.multiple_of(owner_item(x, 0) * ka, ka), ka), :]
        give_ref[dst, :] = gs[pl.ds(pl.multiple_of(owner_item(x, 1) * ka, ka), ka), :].astype(BF)


def ability_gradient(half, d_blocks, bias, response, n_mp, n_item):
    rows, k = half.shape
    cols = response.shape[1]
    shape = jax.ShapeDtypeStruct
    vmem = pl.BlockSpec(memory_space=pltpu.VMEM)
    return pl.pallas_call(
        functools.partial(ability_kernel, n_mp, n_item),
        out_shape=[shape((rows, cols), BF), shape((k // 2, rows), F32), shape((k // 2, rows), BF)],
        in_specs=[vmem] * (3 + n_mp),
        out_specs=[vmem] * 3,
        scratch_shapes=[pltpu.VMEM((k, cols), BF), pltpu.VMEM((k, rows), F32)],
        compiler_params=pltpu.CompilerParams(vmem_limit_bytes=VMEM_BYTES),
        cost_estimate=pl.CostEstimate(
            flops=2 * 2 * rows * cols * k, bytes_accessed=4 * rows * cols, transcendentals=rows * cols
        ),
        name="residual_ability_gradient",
    )(half, *d_blocks, bias, response)


def discrim_kernel(n_mp, at, res, *refs):
    h_out, acc = refs[:n_mp], refs[n_mp]
    kd, cols = h_out[0].shape
    m = lax.axis_index("mp")
    for c in range(0, cols, COL_TILE):
        cr = slice(c, c + COL_TILE)
        acc[:, cr] = jnp.dot(at[...], res[:, cr], preferred_element_type=F32)
    for x in range(n_mp):
        h = acc[pl.ds(pl.multiple_of((m ^ x) * kd, kd), kd), :]
        h_out[x][...] = h.astype(h_out[x].dtype)


def discrim_gradient(at, res, n_mp):
    k, rows = at.shape
    cols = res.shape[1]
    shape = jax.ShapeDtypeStruct
    vmem = pl.BlockSpec(memory_space=pltpu.VMEM)
    return pl.pallas_call(
        functools.partial(discrim_kernel, n_mp),
        out_shape=[shape((k // n_mp, cols), BF if q else F32) for q in range(n_mp)],
        in_specs=[vmem] * 2,
        out_specs=[vmem] * n_mp,
        scratch_shapes=[pltpu.VMEM((k, cols), F32)],
        compiler_params=pltpu.CompilerParams(vmem_limit_bytes=SMALL_VMEM * 2),
        cost_estimate=pl.CostEstimate(
            flops=2 * rows * cols * k, bytes_accessed=2 * rows * cols, transcendentals=0
        ),
        name="discrim_gradient",
    )(at, res)


def pair_kernel(keep_ref, got_ref, *outs):
    ka = outs[0].shape[0]
    for x, out in enumerate(outs):
        rng = slice(x * ka, (x + 1) * ka)
        out[...] = (keep_ref[rng, :] + got_ref[rng, :].astype(F32)).astype(out.dtype)


def pair_sum(keep, got, kinds):
    shape = (keep.shape[0] // len(kinds), keep.shape[1])
    return pl.pallas_call(
        pair_kernel,
        out_shape=[jax.ShapeDtypeStruct(shape, kind) for kind in kinds],
        compiler_params=pltpu.CompilerParams(vmem_limit_bytes=SMALL_VMEM),
        name="core_pair_sum",
    )(keep, got)


def add_kernel(x_ref, y_ref, out_ref):
    out_ref[...] = (x_ref[...] + y_ref[...].astype(F32)).astype(BF)


def add(x, y):
    return pl.pallas_call(
        add_kernel,
        out_shape=jax.ShapeDtypeStruct(x.shape, BF),
        compiler_params=pltpu.CompilerParams(vmem_limit_bytes=SMALL_VMEM),
        cost_estimate=pl.CostEstimate(flops=4000000000, bytes_accessed=8 * x.size, transcendentals=0),
        name="add_partial",
    )(x, y)


def adam_kernel(plan, *refs):
    n_in = sum(n for n, _, _ in plan) + 3 * len(plan)
    ins, outs = refs[:n_in], refs[n_in:]
    for n, scale, rate in plan:
        sums, (x_ref, m_ref, v_ref), ins = ins[:n], ins[n : n + 3], ins[n + 3 :]
        (x_out, m_out, v_out), outs = outs[:3], outs[3:]
        g = sums[0][...]
        for part in sums[1:]:
            g = g + part[...].astype(F32)
        x_out[...], m_out[...], v_out[...] = adam_update(
            x_ref[...], m_ref[...], v_ref[...], g * scale, rate
        )


def adam(*factors):
    plan = [(len(sums), scale, rate) for sums, _, scale, rate in factors]
    operands = [x for sums, state, _, _ in factors for x in (*sums, *state)]
    outs = [jax.ShapeDtypeStruct(x.shape, F32) for _, state, _, _ in factors for x in state]
    return pl.pallas_call(
        functools.partial(adam_kernel, plan),
        out_shape=outs,
        compiler_params=pltpu.CompilerParams(vmem_limit_bytes=SMALL_VMEM),
        name="adam",
    )(*operands)


def shards(response, difficulty, ability, ability_m, ability_v, discrim, discrim_m, discrim_v):
    n_item, n_mp = lax.axis_size("item"), lax.axis_size("mp")
    chips = n_item // 2
    rows, cols = response.shape
    k = discrim.shape[1] * n_mp
    items_total, ckpts_total = cols * n_item, rows * n_mp
    a_t, d_t = ability.T, discrim.T

    def send_chip(x, mask):
        return lax.ppermute(x, "item", swap_item(n_item, 2 * mask))

    def send_core(x):
        return lax.ppermute(x, "item", swap_item(n_item, 1))

    def send_mp(x, masks):
        return lax.ppermute(x, ("mp", "item"), swap_mp(n_mp, n_item, *masks))

    a_bf, d_bf = prepare(a_t, d_t)
    d_blocks = gather(d_bf, mp_basis(n_mp), send_mp)
    mine = [a_bf]
    for b in chip_basis(chips):
        mine += [send_chip(x, b) for x in mine]
        if len(mine) == 2 and n_mp > 2:
            mine[1], d_blocks[2] = lax.optimization_barrier((mine[1], d_blocks[2]))
    theirs = [send_core(x) for x in mine]
    theirs[0], difficulty = lax.optimization_barrier((theirs[0], difficulty))
    bias = (0.5 * difficulty).reshape(1, cols)
    at, half = place_ability(mine + theirs, n_item)
    res, keep, give = ability_gradient(half, d_blocks, bias, response, n_mp, n_item)
    got = send_core(give)
    h = list(discrim_gradient(at, res, n_mp))

    via = [x for x in range(3, chips, 2)]
    got, h[0] = lax.optimization_barrier((got, h[0]))
    g = list(pair_sum(keep, got, [F32 if x == 0 or x ^ 1 in via else BF for x in range(chips)]))
    for x in via:
        g[x ^ 1] = add(g[x ^ 1], send_chip(g[x], 1))
    if via:
        last = max(via) ^ 1
        g[1], g[last] = lax.optimization_barrier((g[1], g[last]))
    h_terms = [h[0]] + [send_mp(h[x], (x, x)) for x in range(1, n_mp)]
    g_terms = [g[0]] + [send_chip(g[x], x) for x in range(chips - 1, 0, -1) if x not in via]
    a_state = (a_t, ability_m.T, ability_v.T)
    d_state = (d_t, discrim_m.T, discrim_v.T)
    d_out = list(adam((h_terms, d_state, 0.5 * math.sqrt(1.0 / ckpts_total), 0.01)))
    g_terms[0], d_out[0] = lax.optimization_barrier((g_terms[0], d_out[0]))
    a_out = adam((g_terms, a_state, 0.5 * math.sqrt(k / items_total), 0.05))
    out = (*a_out, *d_out)
    return tuple(x.T for x in out)


def solution(mesh):
    a_spec, d_spec = P("mp", "item"), P("item", "mp")
    return jax.shard_map(
        shards,
        mesh=mesh,
        in_specs=(a_spec, P("item")) + (a_spec,) * 3 + (d_spec,) * 3,
        out_specs=(a_spec,) * 3 + (d_spec,) * 3,
        check_vma=False,
    )
```
